256 devices in a mesh: mp: 2 (over y_lo), token: 4 (over x), tensor: 32 (over z, y_hi, core).
Axes of the slice: x: 4, y: 4 (y_hi: 2, y_lo: 2; y = y_hi * 2 + y_lo), z: 8, core: 2. Of those that a mesh axis runs over, the one named last changes fastest.
Arguments:
- inputs: bfloat16 [2, 1024, 4096], P('mp', 'token', 'tensor'), may hold values from -6 to 6
- cotangent: bfloat16 [2, 1024, 4096], P('mp', 'token', 'tensor'), may hold values from -6 to 6
- gate_w: bfloat16 [2, 4096, 14336], P('mp', None, 'tensor'), may hold values from -0.09375 to 0.09375
- up_w: bfloat16 [2, 4096, 14336], P('mp', None, 'tensor'), may hold values from -0.09375 to 0.09375
- down_w: bfloat16 [2, 14336, 4096], P('mp', 'tensor'), may hold values from -0.046875 to 0.046875
Outputs:
- input_grad: bfloat16 [2, 1024, 4096], P('mp', 'token', 'tensor')
- merged_gate: bfloat16 [4096, 14336], P(('mp', 'token'), 'tensor')
- merged_up: bfloat16 [4096, 14336], P(('mp', 'token'), 'tensor')
- merged_down: bfloat16 [14336, 4096], P('tensor', ('mp', 'token'))
The draws below stay inside these ranges and needn't reach their ends.
All inputs are finite; a program needn't handle non-finite values.
Results may differ from the reference program's by a relative error of at most 0.02.
Values may be sent and summed in bfloat16 or wider, within the bound.
A program may use at most 192 MiB of HBM per device.

```python
import jax
import jax.numpy as jnp
from jax import lax

D = 4096
FF = 14336
MODELS = 2
TOKENS = 1024
N_TENSOR = 32


def block_scale(own_key, extent, pieces, least, largest):
    factor_of, own = 1.0, jax.random.fold_in(own_key, 6)
    for dim, shards_of in pieces:
        heights = jnp.exp(jax.random.uniform(jax.random.fold_in(own, dim), (shards_of,), jnp.float32, least / len(pieces), largest / len(pieces)))
        factor_of = factor_of * jnp.repeat(heights, extent[dim] // shards_of).reshape([-1 if axis == dim else 1 for axis in range(len(extent))])
    return factor_of


def normal_values(own_key, dims, deviation, limit, shards=(), kind=jnp.bfloat16):
    loudness = block_scale(own_key, dims, shards, -0.22, 0.18) if shards else 1.0
    values = jax.random.normal(own_key, dims, jnp.float32) * deviation * loudness
    return jnp.minimum(jnp.maximum(values, -limit), limit).astype(kind)


def setup_inputs(seed: int = 0) -> dict:
    splits = jax.random.split(jax.random.key(seed), 6)
    inputs = normal_values(splits[0], (MODELS, TOKENS, D), 1.0, 6.0, ((0, 2), (1, 4), (2, 32)))
    cotangent = normal_values(splits[1], (MODELS, TOKENS, D), 1.0, 6.0, ((0, 2), (1, 4), (2, 32)))
    gate_w = normal_values(splits[2], (MODELS, D, FF), D ** -0.5, 0.09375, ((0, 2), (2, 32)))
    up_w = normal_values(splits[3], (MODELS, D, FF), D ** -0.5, 0.09375, ((0, 2), (2, 32)))
    down_w = normal_values(splits[4], (MODELS, FF, D), FF ** -0.5, 0.046875, ((0, 2), (1, 32)))
    return dict(inputs=inputs, cotangent=cotangent, gate_w=gate_w, up_w=up_w, down_w=down_w)


def square_round(value):
    wide = value.astype(jnp.float32)
    return (wide * wide).astype(jnp.bfloat16)

def blockwise_grad(dgate_b, dup_b, wgate, wup):
    cols = FF // N_TENSOR
    tok_count = dgate_b.shape[0]

    def step(total, index):
        start = (index * cols).astype(jnp.int32)
        gpiece = lax.dynamic_slice_in_dim(dgate_b, start, cols, 1)
        upiece = lax.dynamic_slice_in_dim(dup_b, start, cols, 1)
        wgp = lax.dynamic_slice_in_dim(wgate, start, cols, 1)
        wup_piece = lax.dynamic_slice_in_dim(wup, start, cols, 1)
        part = lax.dot_general(gpiece, wgp, (((1,), (1,)), ((), ())), preferred_element_type=jnp.float32)
        part = part + lax.dot_general(upiece, wup_piece, (((1,), (1,)), ((), ())), preferred_element_type=jnp.float32)
        return (total + part.astype(jnp.bfloat16).astype(jnp.float32), None)
    start_total = jnp.zeros((tok_count, D), jnp.float32)
    total, _ = lax.scan(step, start_total, jnp.arange(N_TENSOR, dtype=jnp.int32))
    return total

def reference(inputs, cotangent, gate_w, up_w, down_w):
    grads = []
    num_gate = jnp.zeros((D, FF), jnp.float32)
    num_up = jnp.zeros((D, FF), jnp.float32)
    num_down = jnp.zeros((D, FF), jnp.float32)
    den_gate = jnp.zeros((D, FF), jnp.float32)
    den_up = jnp.zeros((D, FF), jnp.float32)
    den_down = jnp.zeros((D, FF), jnp.float32)
    for model in range(MODELS):
        feats = inputs[model]
        cotan = cotangent[model]
        wgate = gate_w[model]
        wup = up_w[model]
        wdown = down_w[model]
        gate = jnp.dot(feats, wgate, preferred_element_type=jnp.float32)
        upval = jnp.dot(feats, wup, preferred_element_type=jnp.float32)
        sig = jax.nn.sigmoid(gate)
        act = gate * sig
        hidden = (act * upval).astype(jnp.bfloat16)
        dhid = lax.dot_general(cotan, wdown, (((1,), (1,)), ((), ())), preferred_element_type=jnp.float32)
        dgate = dhid * upval * sig * (1.0 + gate * (1.0 - sig))
        dup = dhid * act
        dgate_b = dgate.astype(jnp.bfloat16)
        dup_b = dup.astype(jnp.bfloat16)
        dx = blockwise_grad(dgate_b, dup_b, wgate, wup)
        grads.append(dx.astype(jnp.bfloat16))
        xsq = square_round(feats)
        gsq = square_round(cotan)
        dgsq = (dgate * dgate).astype(jnp.bfloat16)
        dusq = (dup * dup).astype(jnp.bfloat16)
        hsq = square_round(hidden)
        fisher_gate = jnp.dot(xsq.T, dgsq, preferred_element_type=jnp.float32)
        fisher_up = jnp.dot(xsq.T, dusq, preferred_element_type=jnp.float32)
        fisher_down = jnp.dot(gsq.T, hsq, preferred_element_type=jnp.float32)
        num_gate = num_gate + (fisher_gate * wgate.astype(jnp.float32)).astype(jnp.bfloat16).astype(jnp.float32)
        num_up = num_up + (fisher_up * wup.astype(jnp.float32)).astype(jnp.bfloat16).astype(jnp.float32)
        num_down = num_down + (fisher_down * wdown.T.astype(jnp.float32)).astype(jnp.bfloat16).astype(jnp.float32)
        den_gate = den_gate + fisher_gate.astype(jnp.bfloat16).astype(jnp.float32)
        den_up = den_up + fisher_up.astype(jnp.bfloat16).astype(jnp.float32)
        den_down = den_down + fisher_down.astype(jnp.bfloat16).astype(jnp.float32)
    input_grad = jnp.stack(grads, axis=0)
    merged_gate = (num_gate / den_gate).astype(jnp.bfloat16)
    merged_up = (num_up / den_up).astype(jnp.bfloat16)
    merged_down = (num_down / den_down).T.astype(jnp.bfloat16)
    return (input_grad, merged_gate, merged_up, merged_down)
```

```python
import jax
import jax.numpy as jnp
from jax import lax
from jax.experimental import pallas as pl
from jax.experimental.pallas import tpu as pltpu
from jax.sharding import PartitionSpec as P

MESH = pl.DeviceIdType.MESH
BF = jnp.bfloat16
F32 = jnp.float32
TOK = 256
HID = 448
FEAT = 128
ROWS = 512
NZ = 8
NX = 4
NT = (((1,), (1,)), ((), ()))


def kernel(
    inp, cot, gw, uw, dw,
    ig, mg, mu, md,
    xg, rg, xs, hq, gwv, uwv, dwv, wt, wr, fs, fr, nown, down, part, sib, zin, us, vin,
    acc, dgb, dub, sq, ogrd, om, omd,
    load_sem, out_sem, ring_s, ring_r, yx_s, yx_r, sf_s, sf_r, xb_s, xb_r, rf_s, rf_r,
    hq_s, hq_r, w_s, w_r, f_s, f_r, sb_s, sb_r, z_s, z_r, v_s, v_r,
):
    m = lax.axis_index("mp")
    x = lax.axis_index("token")
    k = lax.axis_index("tensor")
    z = k // 4
    yh = (k // 2) % 2
    c = k % 2
    om_ = 1 - m

    def tensor_at(zz, yy, cc):
        return {"tensor": zz * 4 + yy * 2 + cc}

    def wrap(v):
        return (v + 2 * NZ) % NZ

    def remote(src, dst, ssem, rsem, where):
        return pltpu.make_async_remote_copy(
            src_ref=src, dst_ref=dst, send_sem=ssem, recv_sem=rsem, device_id=where, device_id_type=MESH
        )

    sibling = tensor_at(z, yh, 1 - c)
    y_mate = tensor_at(z, 1 - yh, c)
    mp_mate = {"mp": om_}

    loads = [
        pltpu.make_async_copy(inp.at[0], xg.at[0, c, z, yh], load_sem.at[0]),
        pltpu.make_async_copy(cot.at[0], xg.at[1, c, z, yh], load_sem.at[1]),
        pltpu.make_async_copy(gw.at[0], gwv, load_sem.at[2]),
        pltpu.make_async_copy(uw.at[0], uwv, load_sem.at[3]),
        pltpu.make_async_copy(dw.at[0], dwv, load_sem.at[4]),
    ]
    for ld in loads:
        ld.start()

    barrier = pltpu.get_barrier_semaphore()

    def greet(where):
        pl.semaphore_signal(barrier, inc=1, device_id=where, device_id_type=MESH)

    greet(sibling)
    greet(y_mate)
    greet(mp_mate)
    for o in range(1, NX):
        greet({"token": (x + o) % NX})
    for o in range(1, NZ):
        greet(tensor_at((z + o) % NZ, yh, c))
    pl.semaphore_wait(barrier, 3 + (NX - 1) + (NZ - 1))

    def yx_copy(a):
        blk = xg.at[a, c, z, yh]
        return remote(blk, blk, yx_s.at[a], yx_r.at[a], y_mate)

    def ring_copy(a, d, s, u):
        yy = yh if u == 0 else 1 - yh
        zb = wrap(z - (s - 1)) if d == 0 else wrap(z + (s - 1))
        to = wrap(z + 1) if d == 0 else wrap(z - 1)
        blk = xg.at[a, c, zb, yy]
        return remote(blk, blk, ring_s.at[a, d, s, u], ring_r.at[a, d, s, u], tensor_at(to, yh, c))

    def sib_fwd(a, zb, slot):
        blk = xg.at[a, c, zb]
        return remote(blk, blk, sf_s.at[a, slot], sf_r.at[a, slot], sibling)

    def xb_copy(a, zb, slot):
        t = zb % NX
        o = (x - t + NX) % NX - 1
        return remote(
            xg.at[a, c, zb], rg.at[a, c, x, zb // NX], xb_s.at[a, slot], xb_r.at[a, o, zb // NX], {"token": t}
        )

    def xb_start(a, zb, slot):
        @pl.when(zb % NX != x)
        def _():
            xb_copy(a, zb, slot).start()

    def consume(a, zb):
        blk = jnp.concatenate([xg[a, 0, zb, 0], xg[a, 1, zb, 0], xg[a, 0, zb, 1], xg[a, 1, zb, 1]], axis=1)
        at = pl.multiple_of(zb * ROWS, ROWS)
        if a == 0:
            acc[0] += jnp.dot(blk, gwv[pl.ds(at, ROWS), :], preferred_element_type=F32)
            acc[1] += jnp.dot(blk, uwv[pl.ds(at, ROWS), :], preferred_element_type=F32)
        else:
            acc[2] += lax.dot_general(blk, dwv[:, pl.ds(at, ROWS)], NT, preferred_element_type=F32)

    def w_copy(i):
        if i == 2:
            src = dwv.at[:, pl.ds(pl.multiple_of((om_ * NX + x) * ROWS, ROWS), ROWS)]
        else:
            src = wt.at[i, om_]
        return remote(src, wr.at[i], w_s.at[i], w_r.at[i], mp_mate)

    def turn_weights(i, half):
        w = gwv if i == 0 else uwv
        at = pl.multiple_of((half * NX + x) * ROWS, ROWS)
        wt[i, half] = w[pl.ds(at, ROWS), :].T

    for a in range(2):
        loads[a].wait()
    for a in range(2):
        yx_copy(a).start()
        for d in range(2):
            ring_copy(a, d, 1, 0).start()
    acc[...] = jnp.zeros_like(acc)
    loads[4].wait()
    w_copy(2).start()
    for a in range(2):
        yx_copy(a).wait_recv()
        for d in range(2):
            ring_copy(a, d, 1, 1).start()
        sib_fwd(a, z, 0).start()
        xb_start(a, z, 0)
    loads[2].wait()
    loads[3].wait()
    turn_weights(0, om_)
    w_copy(0).start()
    for a in range(2):
        sib_fwd(a, z, 0).wait_recv()
        consume(a, z)

    def ring_step(s, _):
        lo, hi = wrap(z - s), wrap(z + s)
        for a in range(2):
            for u in range(2):
                for d in range(2):
                    ring_copy(a, d, s, u).wait_recv()

                    @pl.when(jnp.logical_or(s < 3, a == d))
                    def _():
                        ring_copy(a, d, s + 1, u).start()
            sib_fwd(a, lo, 2 * s - 1).start()
            sib_fwd(a, hi, 2 * s).start()
            xb_start(a, lo, 2 * s - 1)
            xb_start(a, hi, 2 * s)

        @pl.when(s == 1)
        def _():
            turn_weights(1, om_)
            w_copy(1).start()

        for a in range(2):
            sib_fwd(a, lo, 2 * s - 1).wait_recv()
            consume(a, lo)
            sib_fwd(a, hi, 2 * s).wait_recv()
            consume(a, hi)
        return 0

    lax.fori_loop(1, 4, ring_step, 0)
    far = wrap(z + 4)
    for a in range(2):
        for u in range(2):
            ring_copy(a, a, 4, u).wait_recv()
        sib_fwd(a, far, 7).start()
        xb_start(a, far, 7)
    for a in range(2):
        sib_fwd(a, far, 7).wait_recv()
        consume(a, far)

    def hidden_rows(j, _):
        rows = pl.ds(pl.multiple_of(j * 32, 32), 32)
        gate, up, dh = acc[0, rows, :], acc[1, rows, :], acc[2, rows, :]
        sig = 1.0 / (1.0 + jnp.exp(-gate))
        act = gate * sig
        hid = (act * up).astype(BF).astype(F32)
        dg = dh * up * sig * (1.0 + gate * (1.0 - sig))
        du = dh * act
        dgb[rows, :] = dg.astype(BF)
        dub[rows, :] = du.astype(BF)
        sq[0, rows, :] = dg * dg
        sq[1, rows, :] = du * du
        sq[2, rows, :] = hid * hid
        return 0

    lax.fori_loop(0, TOK // 32, hidden_rows, 0)

    def hq_copy(i, o):
        blk = hq.at[i, x]
        return remote(blk, blk, hq_s.at[i, o - 1], hq_r.at[i, o - 1], {"token": (x + o) % NX})

    for i in range(3):
        hq[i, x] = sq[i].T.astype(BF)
        for o in range(1, NX):
            hq_copy(i, o).start()

    def rg_copy(a, o, half):
        blk = rg.at[a, c, (x + o) % NX, half]
        return remote(blk, blk, rf_s.at[a, o - 1, half], rf_r.at[a, o - 1, half], sibling)

    def rg_landed(a, o, half):
        blk = rg.at[a, c, (x + o) % NX, half]
        return remote(blk, blk, xb_s.at[a, 0], xb_r.at[a, o - 1, half], sibling)

    for a in range(2):
        for o in range(1, NX):
            for half in range(2):
                rg_landed(a, o, half).wait_recv()
                rg_copy(a, o, half).start()

    def grad_block(zb, _):
        at = pl.multiple_of(zb * ROWS, ROWS)
        val = lax.dot_general(dgb[...], gwv[pl.ds(at, ROWS), :], NT, preferred_element_type=F32)
        val += lax.dot_general(dub[...], uwv[pl.ds(at, ROWS), :], NT, preferred_element_type=F32)
        val = val.astype(BF)
        for yy in range(2):
            for cc in range(2):
                part[cc, zb, yy] = val[:, (yy * 2 + cc) * FEAT : (yy * 2 + cc + 1) * FEAT]
        return 0

    lax.fori_loop(0, NZ, grad_block, 0)
    sib_part = remote(part.at[1 - c], sib, sb_s.at[0], sb_r.at[0], sibling)
    sib_part.start()

    def square(v):
        v = v.astype(F32)
        return (v * v).astype(BF)

    for a in range(2):
        for o in range(NX):
            src = (x + o) % NX
            at = pl.multiple_of(src * TOK, TOK)
            for half in range(2):
                if o:
                    rg_copy(a, o, half).wait_recv()
                for yy in range(2):
                    for cc in range(2):
                        v = xg[a, cc, half * NX + x, yy] if o == 0 else rg[a, cc, src, half, yy]
                        lane = (yy * 2 + cc) * FEAT
                        xs[a, half, pl.ds(at, TOK), lane : lane + FEAT] = square(v)

    sib_part.wait_recv()

    def z_copy(o):
        to = (z + o) % NZ
        return remote(sib.at[to], zin.at[z], z_s.at[o - 1], z_r.at[o - 1], tensor_at(to, yh, c))

    def z_landed(o):
        blk = zin.at[wrap(z - o)]
        return remote(blk, blk, z_s.at[o - 1], z_r.at[o - 1], tensor_at(wrap(z - o), yh, c))

    for o in range(1, NZ + 1):
        to = (z + o) % NZ
        sib[to] = (sib[to].astype(F32) + part[c, to].astype(F32)).astype(BF)
        if o < NZ:
            z_copy(o).start()

    for i in range(2):
        turn_weights(i, m)

    def f_copy(i):
        return remote(fs.at[i], fr.at[i], f_s.at[i], f_r.at[i], mp_mate)

    def own_weights(i):
        if i == 2:
            return dwv[:, pl.ds(pl.multiple_of((m * NX + x) * ROWS, ROWS), ROWS)]
        return wt[i, m]

    for i in range(3):
        for o in range(1, NX):
            blk = hq.at[i, (x - o + NX) % NX]
            remote(blk, blk, hq_s.at[i, o - 1], hq_r.at[i, o - 1], {"token": (x - o + NX) % NX}).wait_recv()
        a = 1 if i == 2 else 0
        lhs = jnp.concatenate([hq[i, t] for t in range(NX)], axis=1)
        fs[i] = jnp.dot(lhs, xs[a, om_], preferred_element_type=F32).astype(BF)
        f_copy(i).start()
        fo = jnp.dot(lhs, xs[a, m], preferred_element_type=F32)
        nown[i] = (fo * own_weights(i).astype(F32)).astype(BF)
        down[i] = fo.astype(BF)

    total = sib[z].astype(F32)
    for o in range(1, NZ):
        z_landed(o).wait_recv()
        total += zin[wrap(z - o)].astype(F32)
    us[...] = total.astype(BF)
    v_copy = remote(us.at[1 - yh], vin, v_s.at[0], v_r.at[0], y_mate)
    v_copy.start()

    outs = []
    for i in range(3):
        remote(fr.at[i], fr.at[i], f_s.at[i], f_r.at[i], mp_mate).wait_recv()
        remote(wr.at[i], wr.at[i], w_s.at[i], w_r.at[i], mp_mate).wait_recv()
        if i == 2:
            v_copy.wait_recv()
            ogrd[...] = (us[yh].astype(F32) + vin[...].astype(F32)).astype(BF)
            outs.append(pltpu.make_async_copy(ogrd, ig.at[0], out_sem.at[3]))
            outs[-1].start()
        other = fr[i].astype(F32)
        num = nown[i].astype(F32) + (other * wr[i].astype(F32)).astype(BF).astype(F32)
        merged = num / (down[i].astype(F32) + other)
        if i == 2:
            omd[...] = merged.astype(BF)
        else:
            om[i] = merged.astype(BF).T
        outs.append(pltpu.make_async_copy(om.at[i] if i < 2 else omd, (mg, mu, md)[i], out_sem.at[i]))
        outs[-1].start()

    for a in range(2):
        yx_copy(a).wait_send()
        for u in range(2):
            for d in range(2):
                for s in range(1, 5):
                    if s < 4 or a == d:
                        ring_copy(a, d, s, u).wait_send()
        for slot in range(8):
            sib_fwd(a, z, slot).wait_send()
            zb = wrap(z + (0, -1, 1, -2, 2, -3, 3, 4)[slot])

            @pl.when(zb % NX != x)
            def _():
                xb_copy(a, zb, slot).wait_send()

        for o in range(1, NX):
            for half in range(2):
                rg_copy(a, o, half).wait_send()
    for i in range(3):
        w_copy(i).wait_send()
        f_copy(i).wait_send()
        for o in range(1, NX):
            hq_copy(i, o).wait_send()
    sib_part.wait_send()
    for o in range(1, NZ):
        z_copy(o).wait_send()
    v_copy.wait_send()
    for o in outs:
        o.wait()


def local(*args):
    dma = pltpu.SemaphoreType.DMA
    vm = pltpu.VMEM
    return pl.pallas_call(
        kernel,
        out_shape=(
            jax.ShapeDtypeStruct((1, TOK, FEAT), BF),
            jax.ShapeDtypeStruct((ROWS, HID), BF),
            jax.ShapeDtypeStruct((ROWS, HID), BF),
            jax.ShapeDtypeStruct((HID, ROWS), BF),
        ),
        in_specs=[pl.BlockSpec(memory_space=pl.ANY)] * 5,
        out_specs=[pl.BlockSpec(memory_space=pl.ANY)] * 4,
        scratch_shapes=[
            vm((2, 2, NZ, 2, TOK, FEAT), BF),
            vm((2, 2, NX, 2, 2, TOK, FEAT), BF),
            vm((2, 2, NX * TOK, ROWS), BF),
            vm((3, NX, HID, TOK), BF),
            vm((NZ * ROWS, HID), BF),
            vm((NZ * ROWS, HID), BF),
            vm((HID, NZ * ROWS), BF),
            vm((2, 2, HID, ROWS), BF),
            vm((3, HID, ROWS), BF),
            vm((3, HID, ROWS), BF),
            vm((3, HID, ROWS), BF),
            vm((3, HID, ROWS), BF),
            vm((3, HID, ROWS), BF),
            vm((2, NZ, 2, TOK, FEAT), BF),
            vm((NZ, 2, TOK, FEAT), BF),
            vm((NZ, 2, TOK, FEAT), BF),
            vm((2, TOK, FEAT), BF),
            vm((TOK, FEAT), BF),
            vm((3, TOK, HID), F32),
            vm((TOK, HID), BF),
            vm((TOK, HID), BF),
            vm((3, TOK, HID), F32),
            vm((TOK, FEAT), BF),
            vm((2, ROWS, HID), BF),
            vm((HID, ROWS), BF),
            dma((5,)), dma((4,)),
            dma((2, 2, 5, 2)), dma((2, 2, 5, 2)),
            dma((2,)), dma((2,)),
            dma((2, 8)), dma((2, 8)),
            dma((2, 8)), dma((2, 3, 2)),
            dma((2, 3, 2)), dma((2, 3, 2)),
            dma((3, 3)), dma((3, 3)),
            dma((3,)), dma((3,)),
            dma((3,)), dma((3,)),
            dma((1,)), dma((1,)),
            dma((7,)), dma((7,)),
            dma((1,)), dma((1,)),
        ],
        compiler_params=pltpu.CompilerParams(collective_id=0, has_side_effects=True, vmem_limit_bytes=58 << 20),
        cost_estimate=pl.CostEstimate(flops=7_500_000_000, bytes_accessed=16_000_000, transcendentals=120_000),
        name="fisher_merge",
    )(*args)


def solution(mesh):
    return jax.shard_map(
        local,
        mesh=mesh,
        in_specs=(
            P("mp", "token", "tensor"),
            P("mp", "token", "tensor"),
            P("mp", None, "tensor"),
            P("mp", None, "tensor"),
            P("mp", "tensor", None),
        ),
        out_specs=(
            P("mp", "token", "tensor"),
            P(("mp", "token"), "tensor"),
            P(("mp", "token"), "tensor"),
            P("tensor", ("mp", "token")),
        ),
        check_vma=False,
    )
```

```python
import jax
import jax.numpy as jnp
from jax import lax
from jax.experimental import pallas as pl
from jax.experimental.pallas import tpu as pltpu
from jax.sharding import PartitionSpec as P

MESH = pl.DeviceIdType.MESH
BF = jnp.bfloat16
F32 = jnp.float32
TOK = 256
HID = 448
FEAT = 128
ROWS = 512
NZ = 8
NX = 4
NT = (((1,), (1,)), ((), ()))


def kernel(
    inp, cot, gw, uw, dw,
    ig, mt,
    xg, rg, xs, hq, wv, wr, fs, fr, nown, down, part, sib, zin, us, vin,
    acc, dgt, dut, dgb, dub, ogrd, om,
    load_sem, out_sem, ring_s, ring_r, yx_s, yx_r, sf_s, sf_r, xb_s, xb_r, rf_s, rf_r,
    hq_s, hq_r, w_s, w_r, f_s, f_r, sb_s, sb_r, z_s, z_r, v_s, v_r,
):
    m = lax.axis_index("mp")
    x = lax.axis_index("token")
    k = lax.axis_index("tensor")
    z = k // 4
    yh = (k // 2) % 2
    c = k % 2
    om_ = 1 - m

    def tensor_at(zz, yy, cc):
        return {"tensor": zz * 4 + yy * 2 + cc}

    def wrap(v):
        return (v + 2 * NZ) % NZ

    def remote(src, dst, ssem, rsem, where):
        return pltpu.make_async_remote_copy(
            src_ref=src, dst_ref=dst, send_sem=ssem, recv_sem=rsem, device_id=where, device_id_type=MESH
        )

    sibling = tensor_at(z, yh, 1 - c)
    y_mate = tensor_at(z, 1 - yh, c)
    mp_mate = {"mp": om_}

    loads = [
        pltpu.make_async_copy(inp.at[0], xg.at[0, c, z, yh], load_sem.at[0]),
        pltpu.make_async_copy(cot.at[0], xg.at[1, c, z, yh], load_sem.at[1]),
        pltpu.make_async_copy(gw.at[0], wv.at[0], load_sem.at[2]),
        pltpu.make_async_copy(uw.at[0], wv.at[1], load_sem.at[3]),
        pltpu.make_async_copy(dw.at[0], wv.at[2], load_sem.at[4]),
    ]
    for ld in loads:
        ld.start()

    barrier = pltpu.get_barrier_semaphore()

    def greet(where):
        pl.semaphore_signal(barrier, inc=1, device_id=where, device_id_type=MESH)

    greet(sibling)
    greet(y_mate)
    greet(mp_mate)
    for o in range(1, NX):
        greet({"token": (x + o) % NX})
    for o in range(1, NZ):
        greet(tensor_at((z + o) % NZ, yh, c))
    pl.semaphore_wait(barrier, 3 + (NX - 1) + (NZ - 1))

    def yx_copy(a):
        blk = xg.at[a, c, z, yh]
        return remote(blk, blk, yx_s.at[a], yx_r.at[a], y_mate)

    def ring_copy(a, d, s, u):
        yy = yh if u == 0 else 1 - yh
        zb = wrap(z - (s - 1)) if d == 0 else wrap(z + (s - 1))
        to = wrap(z + 1) if d == 0 else wrap(z - 1)
        blk = xg.at[a, c, zb, yy]
        return remote(blk, blk, ring_s.at[a, d, s, u], ring_r.at[a, d, s, u], tensor_at(to, yh, c))

    def sib_fwd(a, zb, slot):
        blk = xg.at[a, c, zb]
        return remote(blk, blk, sf_s.at[a, slot], sf_r.at[a, slot], sibling)

    def xb_copy(a, zb, slot):
        t = zb % NX
        o = (x - t + NX) % NX - 1
        return remote(
            xg.at[a, c, zb], rg.at[a, c, x, zb // NX], xb_s.at[a, slot], xb_r.at[a, o, zb // NX], {"token": t}
        )

    def xb_start(a, zb, slot):
        @pl.when(zb % NX != x)
        def _():
            xb_copy(a, zb, slot).start()

    def consume(a, zb):
        blk = jnp.concatenate([xg[a, 0, zb, 0], xg[a, 1, zb, 0], xg[a, 0, zb, 1], xg[a, 1, zb, 1]], axis=1)
        at = pl.multiple_of(zb * ROWS, ROWS)
        for i in (0, 1) if a == 0 else (2,):
            acc[i] += lax.dot_general(wv[i, :, pl.ds(at, ROWS)], blk, NT, preferred_element_type=F32)

    def merge_rows(half):
        return pl.ds(pl.multiple_of((half * NX + x) * ROWS, ROWS), ROWS)

    def w_copy(i):
        return remote(wv.at[i, :, merge_rows(om_)], wr.at[i], w_s.at[i], w_r.at[i], mp_mate)

    for a in range(2):
        loads[a].wait()
    for a in range(2):
        yx_copy(a).start()
        for d in range(2):
            ring_copy(a, d, 1, 0).start()
    acc[...] = jnp.zeros_like(acc)
    loads[2].wait()
    w_copy(0).start()
    for a in range(2):
        yx_copy(a).wait_recv()
        for d in range(2):
            ring_copy(a, d, 1, 1).start()
        sib_fwd(a, z, 0).start()
        xb_start(a, z, 0)
    for i in (1, 2):
        loads[2 + i].wait()
        w_copy(i).start()
    for a in range(2):
        sib_fwd(a, z, 0).wait_recv()
        consume(a, z)

    def ring_step(s, _):
        lo, hi = wrap(z - s), wrap(z + s)
        for a in range(2):
            for u in range(2):
                for d in range(2):
                    ring_copy(a, d, s, u).wait_recv()

                    @pl.when(jnp.logical_or(s < 3, a == d))
                    def _():
                        ring_copy(a, d, s + 1, u).start()
            sib_fwd(a, lo, 2 * s - 1).start()
            sib_fwd(a, hi, 2 * s).start()
            xb_start(a, lo, 2 * s - 1)
            xb_start(a, hi, 2 * s)

        for a in range(2):
            sib_fwd(a, lo, 2 * s - 1).wait_recv()
            consume(a, lo)
            sib_fwd(a, hi, 2 * s).wait_recv()
            consume(a, hi)
        return 0

    lax.fori_loop(1, 4, ring_step, 0)
    far = wrap(z + 4)
    for a in range(2):
        for u in range(2):
            ring_copy(a, a, 4, u).wait_recv()
        sib_fwd(a, far, 7).start()
        xb_start(a, far, 7)
    for a in range(2):
        sib_fwd(a, far, 7).wait_recv()
        consume(a, far)

    def hidden_rows(j, _):
        rows = pl.ds(pl.multiple_of(j * 64, 64), 64)
        gate, up, dh = acc[0, rows, :], acc[1, rows, :], acc[2, rows, :]
        sig = 1.0 / (1.0 + jnp.exp(-gate))
        act = gate * sig
        hid = (act * up).astype(BF).astype(F32)
        dg = dh * up * sig * (1.0 + gate * (1.0 - sig))
        du = dh * act
        dgt[rows, :] = dg.astype(BF)
        dut[rows, :] = du.astype(BF)
        hq[0, x, rows, :] = (dg * dg).astype(BF)
        hq[1, x, rows, :] = (du * du).astype(BF)
        hq[2, x, rows, :] = (hid * hid).astype(BF)
        return 0

    lax.fori_loop(0, HID // 64, hidden_rows, 0)

    def hq_copy(i, o):
        blk = hq.at[i, x]
        return remote(blk, blk, hq_s.at[i, o - 1], hq_r.at[i, o - 1], {"token": (x + o) % NX})

    for i in range(3):
        for o in range(1, NX):
            hq_copy(i, o).start()

    def rg_copy(a, o, half):
        blk = rg.at[a, c, (x + o) % NX, half]
        return remote(blk, blk, rf_s.at[a, o - 1, half], rf_r.at[a, o - 1, half], sibling)

    def rg_landed(a, o, half):
        blk = rg.at[a, c, (x + o) % NX, half]
        return remote(blk, blk, xb_s.at[a, 0], xb_r.at[a, o - 1, half], sibling)

    for a in range(2):
        for o in range(1, NX):
            for half in range(2):
                rg_landed(a, o, half).wait_recv()
                rg_copy(a, o, half).start()

    dgb[...] = dgt[...].T
    dub[...] = dut[...].T

    def grad_block(zb, _):
        at = pl.multiple_of(zb * ROWS, ROWS)
        val = jnp.dot(dgb[...], wv[0, :, pl.ds(at, ROWS)], preferred_element_type=F32)
        val += jnp.dot(dub[...], wv[1, :, pl.ds(at, ROWS)], preferred_element_type=F32)
        val = val.astype(BF)
        for yy in range(2):
            for cc in range(2):
                part[cc, zb, yy] = val[:, (yy * 2 + cc) * FEAT : (yy * 2 + cc + 1) * FEAT]
        return 0

    lax.fori_loop(0, NZ, grad_block, 0)
    sib_part = remote(part.at[1 - c], sib, sb_s.at[0], sb_r.at[0], sibling)
    sib_part.start()

    def square(v):
        v = v.astype(F32)
        return (v * v).astype(BF)

    for a in range(2):
        for o in range(NX):
            src = (x + o) % NX
            at = pl.multiple_of(src * TOK, TOK)
            for half in range(2):
                if o:
                    rg_copy(a, o, half).wait_recv()
                for yy in range(2):
                    for cc in range(2):
                        v = xg[a, cc, half * NX + x, yy] if o == 0 else rg[a, cc, src, half, yy]
                        lane = (yy * 2 + cc) * FEAT
                        xs[a, half, pl.ds(at, TOK), lane : lane + FEAT] = square(v)

    sib_part.wait_recv()

    def z_copy(o):
        to = (z + o) % NZ
        return remote(sib.at[to], zin.at[z], z_s.at[o - 1], z_r.at[o - 1], tensor_at(to, yh, c))

    def z_landed(o):
        blk = zin.at[wrap(z - o)]
        return remote(blk, blk, z_s.at[o - 1], z_r.at[o - 1], tensor_at(wrap(z - o), yh, c))

    for o in range(1, NZ + 1):
        to = (z + o) % NZ
        sib[to] = (sib[to].astype(F32) + part[c, to].astype(F32)).astype(BF)
        if o < NZ:
            z_copy(o).start()

    def f_copy(i):
        return remote(fs.at[i], fr.at[i], f_s.at[i], f_r.at[i], mp_mate)

    for i in range(3):
        for o in range(1, NX):
            blk = hq.at[i, (x - o + NX) % NX]
            remote(blk, blk, hq_s.at[i, o - 1], hq_r.at[i, o - 1], {"token": (x - o + NX) % NX}).wait_recv()
        a = 1 if i == 2 else 0
        lhs = jnp.concatenate([hq[i, t] for t in range(NX)], axis=1)
        fs[i] = jnp.dot(lhs, xs[a, om_], preferred_element_type=F32).astype(BF)
        f_copy(i).start()
        fo = jnp.dot(lhs, xs[a, m], preferred_element_type=F32)
        nown[i] = (fo * wv[i, :, merge_rows(m)].astype(F32)).astype(BF)
        down[i] = fo.astype(BF)

    total = sib[z].astype(F32)
    for o in range(1, NZ):
        z_landed(o).wait_recv()
        total += zin[wrap(z - o)].astype(F32)
    us[...] = total.astype(BF)
    v_copy = remote(us.at[1 - yh], vin, v_s.at[0], v_r.at[0], y_mate)
    v_copy.start()

    outs = []
    for i in range(3):
        remote(fr.at[i], fr.at[i], f_s.at[i], f_r.at[i], mp_mate).wait_recv()
        remote(wr.at[i], wr.at[i], w_s.at[i], w_r.at[i], mp_mate).wait_recv()
        if i == 2:
            v_copy.wait_recv()
            ogrd[...] = (us[yh].astype(F32) + vin[...].astype(F32)).astype(BF)
            outs.append(pltpu.make_async_copy(ogrd, ig.at[0], out_sem.at[3]))
            outs[-1].start()
        other = fr[i].astype(F32)
        num = nown[i].astype(F32) + (other * wr[i].astype(F32)).astype(BF).astype(F32)
        merged = num / (down[i].astype(F32) + other)
        om[i] = merged.astype(BF)
        outs.append(pltpu.make_async_copy(om.at[i], mt.at[i], out_sem.at[i]))
        outs[-1].start()

    for a in range(2):
        yx_copy(a).wait_send()
        for u in range(2):
            for d in range(2):
                for s in range(1, 5):
                    if s < 4 or a == d:
                        ring_copy(a, d, s, u).wait_send()
        for slot in range(8):
            sib_fwd(a, z, slot).wait_send()
            zb = wrap(z + (0, -1, 1, -2, 2, -3, 3, 4)[slot])

            @pl.when(zb % NX != x)
            def _():
                xb_copy(a, zb, slot).wait_send()

        for o in range(1, NX):
            for half in range(2):
                rg_copy(a, o, half).wait_send()
    for i in range(3):
        w_copy(i).wait_send()
        f_copy(i).wait_send()
        for o in range(1, NX):
            hq_copy(i, o).wait_send()
    sib_part.wait_send()
    for o in range(1, NZ):
        z_copy(o).wait_send()
    v_copy.wait_send()
    for o in outs:
        o.wait()


def hand_out(ig, mt, ig_out, mg, mu, md, sem):
    copies = [pltpu.make_async_copy(ig, ig_out, sem.at[3])]
    copies += [pltpu.make_async_copy(mt.at[i], (mg, mu, md)[i], sem.at[i]) for i in range(3)]
    for cp in copies:
        cp.start()
    for cp in copies:
        cp.wait()


def local(inputs, cotangent, gate_w, up_w, down_w):
    dma = pltpu.SemaphoreType.DMA
    vm = pltpu.VMEM
    ig, mt = pl.pallas_call(
        kernel,
        out_shape=(
            jax.ShapeDtypeStruct((1, TOK, FEAT), BF),
            jax.ShapeDtypeStruct((3, HID, ROWS), BF),
        ),
        in_specs=[pl.BlockSpec(memory_space=pl.ANY)] * 5,
        out_specs=[pl.BlockSpec(memory_space=pl.ANY)] * 2,
        scratch_shapes=[
            vm((2, 2, NZ, 2, TOK, FEAT), BF),
            vm((2, 2, NX, 2, 2, TOK, FEAT), BF),
            vm((2, 2, NX * TOK, ROWS), BF),
            vm((3, NX, HID, TOK), BF),
            vm((3, HID, NZ * ROWS), BF),
            vm((3, HID, ROWS), BF),
            vm((3, HID, ROWS), BF),
            vm((3, HID, ROWS), BF),
            vm((3, HID, ROWS), BF),
            vm((3, HID, ROWS), BF),
            vm((2, NZ, 2, TOK, FEAT), BF),
            vm((NZ, 2, TOK, FEAT), BF),
            vm((NZ, 2, TOK, FEAT), BF),
            vm((2, TOK, FEAT), BF),
            vm((TOK, FEAT), BF),
            vm((3, HID, TOK), F32),
            vm((HID, TOK), BF),
            vm((HID, TOK), BF),
            vm((TOK, HID), BF),
            vm((TOK, HID), BF),
            vm((TOK, FEAT), BF),
            vm((3, HID, ROWS), BF),
            dma((5,)), dma((4,)),
            dma((2, 2, 5, 2)), dma((2, 2, 5, 2)),
            dma((2,)), dma((2,)),
            dma((2, 8)), dma((2, 8)),
            dma((2, 8)), dma((2, 3, 2)),
            dma((2, 3, 2)), dma((2, 3, 2)),
            dma((3, 3)), dma((3, 3)),
            dma((3,)), dma((3,)),
            dma((3,)), dma((3,)),
            dma((1,)), dma((1,)),
            dma((7,)), dma((7,)),
            dma((1,)), dma((1,)),
        ],
        compiler_params=pltpu.CompilerParams(collective_id=0, has_side_effects=True, vmem_limit_bytes=58 << 20),
        cost_estimate=pl.CostEstimate(flops=7_500_000_000, bytes_accessed=16_000_000, transcendentals=120_000),
        name="fisher_merge",
    )(inputs, cotangent, gate_w.swapaxes(1, 2), up_w.swapaxes(1, 2), down_w)
    ig, mg, mu, md = pl.pallas_call(
        hand_out,
        out_shape=(jax.ShapeDtypeStruct((1, TOK, FEAT), BF),) + (jax.ShapeDtypeStruct((HID, ROWS), BF),) * 3,
        in_specs=[pl.BlockSpec(memory_space=pltpu.VMEM)] * 2,
        out_specs=[pl.BlockSpec(memory_space=pl.ANY)] * 4,
        scratch_shapes=[dma((4,))],
        name="hand_out",
    )(ig, mt)
    return ig, mg.T, mu.T, md


def solution(mesh):
    return jax.shard_map(
        local,
        mesh=mesh,
        in_specs=(
            P("mp", "token", "tensor"),
            P("mp", "token", "tensor"),
            P("mp", None, "tensor"),
            P("mp", None, "tensor"),
            P("mp", "tensor", None),
        ),
        out_specs=(
            P("mp", "token", "tensor"),
            P(("mp", "token"), "tensor"),
            P(("mp", "token"), "tensor"),
            P("tensor", ("mp", "token")),
        ),
        check_vma=False,
    )
```

```python
import jax
import jax.numpy as jnp
from jax import lax
from jax.experimental import pallas as pl
from jax.experimental.pallas import tpu as pltpu
from jax.sharding import PartitionSpec as P

MESH = pl.DeviceIdType.MESH
BF = jnp.bfloat16
F32 = jnp.float32
TOK = 256
HID = 448
FEAT = 128
ROWS = 512
NZ = 8
NX = 4
HALF = HID // 2
PIECES = 6
LATE = 3
NT = (((1,), (1,)), ((), ()))


def kernel(
    inp, cot, gw, uw, dw,
    ig, mt,
    xg, rg, xs, hq, wv, wr, fs, fr, nown, down, part, sib, zin, us, vin,
    acc, dgt, dut, dgb, dub,
    load_sem, ring_s, ring_r, yx_s, yx_r, sf_s, sf_r, xb_s, xb_r, rf_s, rf_r,
    hq_s, hq_r, w_s, w_r, f_s, f_r, sb_s, sb_r, z_s, z_r, v_s, v_r,
):
    m = lax.axis_index("mp")
    x = lax.axis_index("token")
    k = lax.axis_index("tensor")
    z = k // 4
    yh = (k // 2) % 2
    c = k % 2
    om_ = 1 - m

    def tensor_at(zz, yy, cc):
        return {"tensor": zz * 4 + yy * 2 + cc}

    def wrap(v):
        return (v + 2 * NZ) % NZ

    def remote(src, dst, ssem, rsem, where):
        return pltpu.make_async_remote_copy(
            src_ref=src, dst_ref=dst, send_sem=ssem, recv_sem=rsem, device_id=where, device_id_type=MESH
        )

    sibling = tensor_at(z, yh, 1 - c)
    y_mate = tensor_at(z, 1 - yh, c)
    mp_mate = {"mp": om_}

    loads = [
        pltpu.make_async_copy(inp.at[0], xg.at[0, c, z, yh], load_sem.at[0]),
        pltpu.make_async_copy(cot.at[0], xg.at[1, c, z, yh], load_sem.at[1]),
        pltpu.make_async_copy(gw.at[0], wv.at[0], load_sem.at[2]),
        pltpu.make_async_copy(uw.at[0], wv.at[1], load_sem.at[3]),
        pltpu.make_async_copy(dw.at[0], wv.at[2], load_sem.at[4]),
    ]
    for ld in loads:
        ld.start()

    barrier = pltpu.get_barrier_semaphore()

    def greet(where):
        pl.semaphore_signal(barrier, inc=1, device_id=where, device_id_type=MESH)

    greet(sibling)
    greet(y_mate)
    greet(mp_mate)
    for o in range(1, NX):
        greet({"token": (x + o) % NX})
    for o in (1, NZ - 1):
        greet(tensor_at((z + o) % NZ, yh, c))
    pl.semaphore_wait(barrier, 3 + (NX - 1) + 2)

    def yx_copy(a):
        blk = xg.at[a, c, z, yh]
        return remote(blk, blk, yx_s.at[a], yx_r.at[a], y_mate)

    def ring_copy(a, d, s, u):
        yy = yh if u == 0 else 1 - yh
        zb = wrap(z - (s - 1)) if d == 0 else wrap(z + (s - 1))
        to = wrap(z + 1) if d == 0 else wrap(z - 1)
        blk = xg.at[a, c, zb, yy]
        return remote(blk, blk, ring_s.at[a, d, s, u], ring_r.at[a, d, s, u], tensor_at(to, yh, c))

    def sib_fwd(a, zb, slot):
        blk = xg.at[a, c, zb]
        return remote(blk, blk, sf_s.at[a, slot], sf_r.at[a, slot], sibling)

    def xb_copy(a, zb, slot):
        t = zb % NX
        o = (x - t + NX) % NX - 1
        return remote(
            xg.at[a, c, zb], rg.at[a, c, x, zb // NX], xb_s.at[a, slot], xb_r.at[a, o, zb // NX], {"token": t}
        )

    def xb_start(a, zb, slot):
        @pl.when(zb % NX != x)
        def _():
            xb_copy(a, zb, slot).start()

    def consume(a, zb):
        blk = jnp.concatenate([xg[a, 0, zb, 0], xg[a, 1, zb, 0], xg[a, 0, zb, 1], xg[a, 1, zb, 1]], axis=1)
        at = pl.multiple_of(zb * ROWS, ROWS)
        for i in (0, 1) if a == 0 else (2,):
            acc[i] += lax.dot_general(wv[i, :, pl.ds(at, ROWS)], blk, NT, preferred_element_type=F32)

    def merge_rows(half):
        return pl.ds(pl.multiple_of((half * NX + x) * ROWS, ROWS), ROWS)

    def w_copy(i):
        return remote(wv.at[i, :, merge_rows(om_)], wr.at[i], w_s.at[i], w_r.at[i], mp_mate)

    for a in range(2):
        loads[a].wait()
    for a in range(2):
        yx_copy(a).start()
        for d in range(2):
            ring_copy(a, d, 1, 0).start()
    acc[...] = jnp.zeros_like(acc)
    loads[2].wait()
    w_copy(0).start()
    for a in range(2):
        yx_copy(a).wait_recv()
        for d in range(2):
            ring_copy(a, d, 1, 1).start()
        sib_fwd(a, z, 0).start()
        xb_start(a, z, 0)
    for i in (1, 2):
        loads[2 + i].wait()
        w_copy(i).start()
    for a in range(2):
        sib_fwd(a, z, 0).wait_recv()
        consume(a, z)

    def ring_step(s, _):
        lo, hi = wrap(z - s), wrap(z + s)
        for a in range(2):
            for u in range(2):
                for d in range(2):
                    ring_copy(a, d, s, u).wait_recv()

                    @pl.when(jnp.logical_or(s < 3, a == d))
                    def _():
                        ring_copy(a, d, s + 1, u).start()
            sib_fwd(a, lo, 2 * s - 1).start()
            sib_fwd(a, hi, 2 * s).start()
            if a == 0:
                xb_start(a, lo, 2 * s - 1)
                xb_start(a, hi, 2 * s)
            else:

                @pl.when(s < LATE)
                def _():
                    xb_start(a, lo, 2 * s - 1)
                    xb_start(a, hi, 2 * s)


        for a in range(2):
            sib_fwd(a, lo, 2 * s - 1).wait_recv()
            consume(a, lo)
            sib_fwd(a, hi, 2 * s).wait_recv()
            consume(a, hi)
        return 0

    lax.fori_loop(1, 4, ring_step, 0)
    far = wrap(z + 4)
    for a in range(2):
        for u in range(2):
            ring_copy(a, a, 4, u).wait_recv()
        sib_fwd(a, far, 7).start()
        if a == 0:
            xb_start(a, far, 7)
    for a in range(2):
        sib_fwd(a, far, 7).wait_recv()
        consume(a, far)

    def hidden_rows(j, _):
        rows = pl.ds(pl.multiple_of(j * 64, 64), 64)
        gate, up, dh = acc[0, rows, :], acc[1, rows, :], acc[2, rows, :]
        sig = 1.0 / (1.0 + jnp.exp(-gate))
        act = gate * sig
        hid = (act * up).astype(BF).astype(F32)
        dg = dh * up * sig * (1.0 + gate * (1.0 - sig))
        du = dh * act
        dgt[rows, :] = dg.astype(BF)
        dut[rows, :] = du.astype(BF)
        hq[0, x, rows, :] = (dg * dg).astype(BF)
        hq[1, x, rows, :] = (du * du).astype(BF)
        hq[2, x, rows, :] = (hid * hid).astype(BF)
        return 0

    lax.fori_loop(0, HID // 64, hidden_rows, 0)

    def piece(j):
        return j // 2, pl.ds(j % 2 * HALF, HALF)

    def hq_copy(j, d, hops):
        i, units = piece(j)
        src = x
        if hops:
            src = (x + NX - 1) % NX if d == 0 else (x + 1) % NX
            units = pl.ds(j % 2 * HALF + d * (HALF // 2), HALF // 2)
        blk = hq.at[i, src, units]
        to = (x + 1) % NX if d == 0 else (x + NX - 1) % NX
        return remote(blk, blk, hq_s.at[j, d, hops], hq_r.at[j, d, hops], {"token": to})

    def hq_send(j):
        for d in range(2):
            hq_copy(j, d, 0).start()

    def hq_relay(j):
        for d in range(2):
            hq_copy(j, d, 0).wait_recv()
            hq_copy(j, d, 1).start()

    hq_send(0)

    def rg_copy(a, o, half):
        blk = rg.at[a, c, (x + o) % NX, half]
        return remote(blk, blk, rf_s.at[a, o - 1, half], rf_r.at[a, o - 1, half], sibling)

    def rg_landed(a, o, half):
        blk = rg.at[a, c, (x + o) % NX, half]
        return remote(blk, blk, xb_s.at[a, 0], xb_r.at[a, o - 1, half], sibling)

    def rg_pass(a):
        for o in range(1, NX):
            for half in range(2):
                rg_landed(a, o, half).wait_recv()
                rg_copy(a, o, half).start()

    def square(v):
        v = v.astype(F32)
        return (v * v).astype(BF)

    def squares(a):
        for o in range(NX):
            src = (x + o) % NX
            at = pl.multiple_of(src * TOK, TOK)
            for half in range(2):
                if o:
                    rg_copy(a, o, half).wait_recv()
                for yy in range(2):
                    for cc in range(2):
                        v = xg[a, cc, half * NX + x, yy] if o == 0 else rg[a, cc, src, half, yy]
                        lane = (yy * 2 + cc) * FEAT
                        xs[a, half, pl.ds(at, TOK), lane : lane + FEAT] = square(v)

    def f_copy(j):
        i, units = piece(j)
        return remote(fs.at[i, units], fr.at[i, units], f_s.at[j], f_r.at[j], mp_mate)

    def hq_wait(j):
        for d in range(2):
            hq_copy(j, d, 1).wait_recv()

    def fisher(j):
        i, units = piece(j)
        a = 1 if i == 2 else 0
        lhs = jnp.concatenate([hq[i, t, units] for t in range(NX)], axis=1)
        fs[i, units] = jnp.dot(lhs, xs[a, om_], preferred_element_type=F32).astype(BF)
        f_copy(j).start()
        fo = jnp.dot(lhs, xs[a, m], preferred_element_type=F32)
        nown[i, units] = (fo * wv[i, units, merge_rows(m)].astype(F32)).astype(BF)
        down[i, units] = fo.astype(BF)

    dgb[...] = dgt[...].T
    dub[...] = dut[...].T

    def grad_block(zb, _):
        at = pl.multiple_of(zb * ROWS, ROWS)
        val = jnp.dot(dgb[...], wv[0, :, pl.ds(at, ROWS)], preferred_element_type=F32)
        val += jnp.dot(dub[...], wv[1, :, pl.ds(at, ROWS)], preferred_element_type=F32)
        val = val.astype(BF)
        for yy in range(2):
            for cc in range(2):
                part[cc, zb, yy] = val[:, (yy * 2 + cc) * FEAT : (yy * 2 + cc + 1) * FEAT]
        return 0

    lax.fori_loop(0, NZ, grad_block, 0)
    sib_part = remote(part.at[1 - c], sib, sb_s.at[0], sb_r.at[0], sibling)
    sib_part.start()
    hq_send(1)
    hq_relay(0)
    for s in range(LATE, 5):
        for slot in (2 * s - 1, 2 * s) if s < 4 else (7,):
            xb_start(1, wrap(z - s if slot % 2 else z + s), slot)
    rg_pass(0)
    squares(0)
    hq_send(2)
    hq_relay(1)
    hq_wait(0)
    fisher(0)

    def z_copy(o):
        to = (z + o) % NZ
        return remote(sib.at[to], zin.at[z], z_s.at[o - 1], z_r.at[o - 1], tensor_at(to, yh, c))

    def z_landed(o):
        blk = zin.at[wrap(z - o)]
        return remote(blk, blk, z_s.at[o - 1], z_r.at[o - 1], tensor_at(wrap(z - o), yh, c))

    sib_part.wait_recv()
    for o in range(1, NZ + 1):
        to = (z + o) % NZ
        sib[to] = (sib[to].astype(F32) + part[c, to].astype(F32)).astype(BF)
        if o < NZ:
            z_copy(o).start()

    hq_send(3)
    hq_relay(2)
    hq_wait(1)
    fisher(1)
    hq_send(4)
    hq_relay(3)
    hq_wait(2)
    fisher(2)
    hq_send(5)
    hq_relay(4)
    rg_pass(1)
    squares(1)
    hq_wait(3)
    fisher(3)
    hq_relay(5)
    hq_wait(4)
    fisher(4)
    hq_wait(5)
    fisher(5)

    total = sib[z].astype(F32)
    for o in range(1, NZ):
        z_landed(o).wait_recv()
        total += zin[wrap(z - o)].astype(F32)
    us[...] = total.astype(BF)
    v_copy = remote(us.at[1 - yh], vin, v_s.at[0], v_r.at[0], y_mate)
    v_copy.start()

    for i in range(3):
        remote(wr.at[i], wr.at[i], w_s.at[i], w_r.at[i], mp_mate).wait_recv()
    for j in range(PIECES):
        i, units = piece(j)
        f_copy(j).wait_recv()
        if j == PIECES - 1:
            v_copy.wait_recv()
            ig[0] = (us[yh].astype(F32) + vin[...].astype(F32)).astype(BF)
        other = fr[i, units].astype(F32)
        num = nown[i, units].astype(F32) + (other * wr[i, units].astype(F32)).astype(BF).astype(F32)
        mt[i, units] = (num / (down[i, units].astype(F32) + other)).astype(BF)

    for a in range(2):
        yx_copy(a).wait_send()
        for u in range(2):
            for d in range(2):
                for s in range(1, 5):
                    if s < 4 or a == d:
                        ring_copy(a, d, s, u).wait_send()
        for slot in range(8):
            sib_fwd(a, z, slot).wait_send()
            zb = wrap(z + (0, -1, 1, -2, 2, -3, 3, 4)[slot])

            @pl.when(zb % NX != x)
            def _():
                xb_copy(a, zb, slot).wait_send()

        for o in range(1, NX):
            for half in range(2):
                rg_copy(a, o, half).wait_send()
    for i in range(3):
        w_copy(i).wait_send()
    for j in range(PIECES):
        f_copy(j).wait_send()
        for d in range(2):
            for hops in range(2):
                hq_copy(j, d, hops).wait_send()
    sib_part.wait_send()
    for o in range(1, NZ):
        z_copy(o).wait_send()
    v_copy.wait_send()


def hand_out(ig, mt, ig_out, mg, mu, md, sem):
    copies = [pltpu.make_async_copy(ig, ig_out, sem.at[3])]
    copies += [pltpu.make_async_copy(mt.at[i], (mg, mu, md)[i], sem.at[i]) for i in range(3)]
    for cp in copies:
        cp.start()
    for cp in copies:
        cp.wait()


def local(inputs, cotangent, gate_w, up_w, down_w):
    dma = pltpu.SemaphoreType.DMA
    vm = pltpu.VMEM
    ig, mt = pl.pallas_call(
        kernel,
        out_shape=(
            vm((1, TOK, FEAT), BF),
            vm((3, HID, ROWS), BF),
        ),
        in_specs=[pl.BlockSpec(memory_space=pl.ANY)] * 5,
        out_specs=[pl.BlockSpec(memory_space=pltpu.VMEM)] * 2,
        scratch_shapes=[
            vm((2, 2, NZ, 2, TOK, FEAT), BF),
            vm((2, 2, NX, 2, 2, TOK, FEAT), BF),
            vm((2, 2, NX * TOK, ROWS), BF),
            vm((3, NX, HID, TOK), BF),
            vm((3, HID, NZ * ROWS), BF),
            vm((3, HID, ROWS), BF),
            vm((3, HID, ROWS), BF),
            vm((3, HID, ROWS), BF),
            vm((3, HID, ROWS), BF),
            vm((3, HID, ROWS), BF),
            vm((2, NZ, 2, TOK, FEAT), BF),
            vm((NZ, 2, TOK, FEAT), BF),
            vm((NZ, 2, TOK, FEAT), BF),
            vm((2, TOK, FEAT), BF),
            vm((TOK, FEAT), BF),
            vm((3, HID, TOK), F32),
            vm((HID, TOK), BF),
            vm((HID, TOK), BF),
            vm((TOK, HID), BF),
            vm((TOK, HID), BF),
            dma((5,)),
            dma((2, 2, 5, 2)), dma((2, 2, 5, 2)),
            dma((2,)), dma((2,)),
            dma((2, 8)), dma((2, 8)),
            dma((2, 8)), dma((2, 3, 2)),
            dma((2, 3, 2)), dma((2, 3, 2)),
            dma((6, 2, 2)), dma((6, 2, 2)),
            dma((3,)), dma((3,)),
            dma((6,)), dma((6,)),
            dma((1,)), dma((1,)),
            dma((7,)), dma((7,)),
            dma((1,)), dma((1,)),
        ],
        compiler_params=pltpu.CompilerParams(collective_id=0, has_side_effects=True, vmem_limit_bytes=58 << 20),
        cost_estimate=pl.CostEstimate(flops=7_500_000_000, bytes_accessed=16_000_000, transcendentals=120_000),
        name="fisher_merge",
    )(inputs, cotangent, gate_w.swapaxes(1, 2), up_w.swapaxes(1, 2), down_w)
    ig, mg, mu, md = pl.pallas_call(
        hand_out,
        out_shape=(jax.ShapeDtypeStruct((1, TOK, FEAT), BF),) + (jax.ShapeDtypeStruct((HID, ROWS), BF),) * 3,
        in_specs=[pl.BlockSpec(memory_space=pltpu.VMEM)] * 2,
        out_specs=[pl.BlockSpec(memory_space=pl.ANY)] * 4,
        scratch_shapes=[dma((4,))],
        name="hand_out",
    )(*(pltpu.with_memory_space_constraint(v, pltpu.VMEM) for v in (ig, mt)))
    return ig, mg.T, mu.T, md


def solution(mesh):
    return jax.shard_map(
        local,
        mesh=mesh,
        in_specs=(
            P("mp", "token", "tensor"),
            P("mp", "token", "tensor"),
            P("mp", None, "tensor"),
            P("mp", None, "tensor"),
            P("mp", "tensor", None),
        ),
        out_specs=(
            P("mp", "token", "tensor"),
            P(("mp", "token"), "tensor"),
            P(("mp", "token"), "tensor"),
            P("tensor", ("mp", "token")),
        ),
        check_vma=False,
    )
```

```python
import jax
import jax.numpy as jnp
from jax import lax
from jax.experimental import pallas as pl
from jax.experimental.pallas import tpu as pltpu
from jax.sharding import PartitionSpec as P

MESH = pl.DeviceIdType.MESH
BF = jnp.bfloat16
F32 = jnp.float32
TOK = 256
HID = 448
FEAT = 128
ROWS = 512
NZ = 8
NX = 4
HALF = HID // 2
PIECES = 6
MERGED = 4
LATE = 3
NT = (((1,), (1,)), ((), ()))


def kernel(
    inp, cot, gw, uw, dw,
    ig, mt,
    xg, rg, xs, hq, wv, wr, fs, fr, nown, down, part, sib, zin, us, vin,
    acc, dgt, dut, dgb, dub,
    load_sem, ring_s, ring_r, yx_s, yx_r, sf_s, sf_r, xb_s, xb_r, rf_s, rf_r,
    hq_s, hq_r, w_s, w_r, f_s, f_r, sb_s, sb_r, z_s, z_r, v_s, v_r,
):
    m = lax.axis_index("mp")
    x = lax.axis_index("token")
    k = lax.axis_index("tensor")
    z = k // 4
    yh = (k // 2) % 2
    c = k % 2
    om_ = 1 - m

    def tensor_at(zz, yy, cc):
        return {"tensor": zz * 4 + yy * 2 + cc}

    def wrap(v):
        return (v + 2 * NZ) % NZ

    def remote(src, dst, ssem, rsem, where):
        return pltpu.make_async_remote_copy(
            src_ref=src, dst_ref=dst, send_sem=ssem, recv_sem=rsem, device_id=where, device_id_type=MESH
        )

    sibling = tensor_at(z, yh, 1 - c)
    y_mate = tensor_at(z, 1 - yh, c)
    mp_mate = {"mp": om_}

    loads = [
        pltpu.make_async_copy(inp.at[0], xg.at[0, c, z, yh], load_sem.at[0]),
        pltpu.make_async_copy(cot.at[0], xg.at[1, c, z, yh], load_sem.at[1]),
        pltpu.make_async_copy(gw.at[0], wv.at[0], load_sem.at[2]),
        pltpu.make_async_copy(uw.at[0], wv.at[1], load_sem.at[3]),
        pltpu.make_async_copy(dw.at[0], wv.at[2], load_sem.at[4]),
    ]
    for ld in loads:
        ld.start()

    barrier = pltpu.get_barrier_semaphore()

    def greet(where):
        pl.semaphore_signal(barrier, inc=1, device_id=where, device_id_type=MESH)

    greet(sibling)
    greet(y_mate)
    greet(mp_mate)
    for o in range(1, NX):
        greet({"token": (x + o) % NX})
    for o in (1, NZ - 1):
        greet(tensor_at((z + o) % NZ, yh, c))
    pl.semaphore_wait(barrier, 3 + (NX - 1) + 2)

    def yx_copy(a):
        blk = xg.at[a, c, z, yh]
        return remote(blk, blk, yx_s.at[a], yx_r.at[a], y_mate)

    def ring_copy(a, d, s, u):
        yy = yh if u == 0 else 1 - yh
        zb = wrap(z - (s - 1)) if d == 0 else wrap(z + (s - 1))
        to = wrap(z + 1) if d == 0 else wrap(z - 1)
        blk = xg.at[a, c, zb, yy]
        return remote(blk, blk, ring_s.at[a, d, s, u], ring_r.at[a, d, s, u], tensor_at(to, yh, c))

    def sib_fwd(a, zb, slot):
        blk = xg.at[a, c, zb]
        return remote(blk, blk, sf_s.at[a, slot], sf_r.at[a, slot], sibling)

    def xb_copy(a, zb, slot):
        t = zb % NX
        o = (x - t + NX) % NX - 1
        return remote(
            xg.at[a, c, zb], rg.at[a, c, x, zb // NX], xb_s.at[a, slot], xb_r.at[a, o, zb // NX], {"token": t}
        )

    def xb_start(a, zb, slot):
        @pl.when(zb % NX != x)
        def _():
            xb_copy(a, zb, slot).start()

    def consume(a, zb):
        blk = jnp.concatenate([xg[a, 0, zb, 0], xg[a, 1, zb, 0], xg[a, 0, zb, 1], xg[a, 1, zb, 1]], axis=1)
        at = pl.multiple_of(zb * ROWS, ROWS)
        for i in (0, 1) if a == 0 else (2,):
            acc[i] += lax.dot_general(wv[i, :, pl.ds(at, ROWS)], blk, NT, preferred_element_type=F32)

    def merge_rows(half):
        return pl.ds(pl.multiple_of((half * NX + x) * ROWS, ROWS), ROWS)

    def w_copy(i):
        return remote(wv.at[i, :, merge_rows(om_)], wr.at[i], w_s.at[i], w_r.at[i], mp_mate)

    for a in range(2):
        loads[a].wait()
    for a in range(2):
        yx_copy(a).start()
        for d in range(2):
            ring_copy(a, d, 1, 0).start()
    acc[...] = jnp.zeros_like(acc)
    loads[2].wait()
    w_copy(0).start()
    for a in range(2):
        yx_copy(a).wait_recv()
        for d in range(2):
            ring_copy(a, d, 1, 1).start()
        sib_fwd(a, z, 0).start()
        xb_start(a, z, 0)
    for i in (1, 2):
        loads[2 + i].wait()
        w_copy(i).start()
    for a in range(2):
        sib_fwd(a, z, 0).wait_recv()
        consume(a, z)

    def ring_step(s, _):
        lo, hi = wrap(z - s), wrap(z + s)
        for a in range(2):
            for u in range(2):
                for d in range(2):
                    ring_copy(a, d, s, u).wait_recv()

                    @pl.when(jnp.logical_or(s < 3, a == d))
                    def _():
                        ring_copy(a, d, s + 1, u).start()
            sib_fwd(a, lo, 2 * s - 1).start()
            sib_fwd(a, hi, 2 * s).start()
            if a == 0:
                xb_start(a, lo, 2 * s - 1)
                xb_start(a, hi, 2 * s)
            else:

                @pl.when(s < LATE)
                def _():
                    xb_start(a, lo, 2 * s - 1)
                    xb_start(a, hi, 2 * s)


        for a in range(2):
            sib_fwd(a, lo, 2 * s - 1).wait_recv()
            consume(a, lo)
            sib_fwd(a, hi, 2 * s).wait_recv()
            consume(a, hi)
        return 0

    lax.fori_loop(1, 4, ring_step, 0)
    far = wrap(z + 4)
    for a in range(2):
        for u in range(2):
            ring_copy(a, a, 4, u).wait_recv()
        sib_fwd(a, far, 7).start()
        if a == 0:
            xb_start(a, far, 7)
    for a in range(2):
        sib_fwd(a, far, 7).wait_recv()
        consume(a, far)

    def hidden_rows(j, _):
        rows = pl.ds(pl.multiple_of(j * 64, 64), 64)
        gate, up, dh = acc[0, rows, :], acc[1, rows, :], acc[2, rows, :]
        sig = 1.0 / (1.0 + jnp.exp(-gate))
        act = gate * sig
        hid = (act * up).astype(BF).astype(F32)
        dg = dh * up * sig * (1.0 + gate * (1.0 - sig))
        du = dh * act
        dgt[rows, :] = dg.astype(BF)
        dut[rows, :] = du.astype(BF)
        hq[0, x, rows, :] = (dg * dg).astype(BF)
        hq[1, x, rows, :] = (du * du).astype(BF)
        hq[2, x, rows, :] = (hid * hid).astype(BF)
        return 0

    lax.fori_loop(0, HID // 64, hidden_rows, 0)

    def piece(j):
        return j // 2, pl.ds(j % 2 * HALF, HALF)

    def hq_copy(j, d, hops):
        i, units = piece(j)
        src = x
        if hops:
            src = (x + NX - 1) % NX if d == 0 else (x + 1) % NX
            units = pl.ds(j % 2 * HALF + d * (HALF // 2), HALF // 2)
        blk = hq.at[i, src, units]
        to = (x + 1) % NX if d == 0 else (x + NX - 1) % NX
        return remote(blk, blk, hq_s.at[j, d, hops], hq_r.at[j, d, hops], {"token": to})

    def hq_send(j):
        for d in range(2):
            hq_copy(j, d, 0).start()

    def hq_relay(j):
        for d in range(2):
            hq_copy(j, d, 0).wait_recv()
            hq_copy(j, d, 1).start()

    def merge(j):
        i, units = piece(j)
        if j % 2 == 0:
            remote(wr.at[i], wr.at[i], w_s.at[i], w_r.at[i], mp_mate).wait_recv()
        f_copy(j).wait_recv()
        other = fr[i, units].astype(F32)
        num = nown[i, units].astype(F32) + (other * wr[i, units].astype(F32)).astype(BF).astype(F32)
        mt[i, units] = (num / (down[i, units].astype(F32) + other)).astype(BF)

    hq_send(0)
    for s in range(LATE, 5):
        for slot in (2 * s - 1, 2 * s) if s < 4 else (7,):
            xb_start(1, wrap(z - s if slot % 2 else z + s), slot)

    def rg_copy(a, o, half):
        blk = rg.at[a, c, (x + o) % NX, half]
        return remote(blk, blk, rf_s.at[a, o - 1, half], rf_r.at[a, o - 1, half], sibling)

    def rg_landed(a, o, half):
        blk = rg.at[a, c, (x + o) % NX, half]
        return remote(blk, blk, xb_s.at[a, 0], xb_r.at[a, o - 1, half], sibling)

    def rg_pass(a):
        for o in range(1, NX):
            for half in range(2):
                rg_landed(a, o, half).wait_recv()
                rg_copy(a, o, half).start()

    def square(v):
        v = v.astype(F32)
        return (v * v).astype(BF)

    def squares(a):
        for o in range(NX):
            src = (x + o) % NX
            at = pl.multiple_of(src * TOK, TOK)
            for half in range(2):
                if o:
                    rg_copy(a, o, half).wait_recv()
                for yy in range(2):
                    for cc in range(2):
                        v = xg[a, cc, half * NX + x, yy] if o == 0 else rg[a, cc, src, half, yy]
                        lane = (yy * 2 + cc) * FEAT
                        xs[a, half, pl.ds(at, TOK), lane : lane + FEAT] = square(v)

    def f_copy(j):
        i, units = piece(j)
        return remote(fs.at[i, units], fr.at[i, units], f_s.at[j], f_r.at[j], mp_mate)

    def hq_wait(j):
        for d in range(2):
            hq_copy(j, d, 1).wait_recv()

    def fisher(j):
        i, units = piece(j)
        a = 1 if i == 2 else 0
        lhs = jnp.concatenate([hq[i, t, units] for t in range(NX)], axis=1)
        fs[i, units] = jnp.dot(lhs, xs[a, om_], preferred_element_type=F32).astype(BF)
        f_copy(j).start()
        fo = jnp.dot(lhs, xs[a, m], preferred_element_type=F32)
        nown[i, units] = (fo * wv[i, units, merge_rows(m)].astype(F32)).astype(BF)
        down[i, units] = fo.astype(BF)

    dgb[...] = dgt[...].T
    dub[...] = dut[...].T

    def grad_block(zb, _):
        at = pl.multiple_of(zb * ROWS, ROWS)
        val = jnp.dot(dgb[...], wv[0, :, pl.ds(at, ROWS)], preferred_element_type=F32)
        val += jnp.dot(dub[...], wv[1, :, pl.ds(at, ROWS)], preferred_element_type=F32)
        val = val.astype(BF)
        for yy in range(2):
            for cc in range(2):
                part[cc, zb, yy] = val[:, (yy * 2 + cc) * FEAT : (yy * 2 + cc + 1) * FEAT]
        return 0

    lax.fori_loop(0, NZ, grad_block, 0)
    sib_part = remote(part.at[1 - c], sib, sb_s.at[0], sb_r.at[0], sibling)
    sib_part.start()
    hq_send(1)
    hq_relay(0)
    rg_pass(0)
    squares(0)
    def z_copy(o):
        to = (z + o) % NZ
        return remote(sib.at[to], zin.at[z], z_s.at[o - 1], z_r.at[o - 1], tensor_at(to, yh, c))

    def z_landed(o):
        blk = zin.at[wrap(z - o)]
        return remote(blk, blk, z_s.at[o - 1], z_r.at[o - 1], tensor_at(wrap(z - o), yh, c))

    hq_send(2)
    hq_relay(1)
    sib_part.wait_recv()
    for o in range(1, NZ + 1):
        to = (z + o) % NZ
        sib[to] = (sib[to].astype(F32) + part[c, to].astype(F32)).astype(BF)
        if o < NZ:
            z_copy(o).start()

    hq_wait(0)
    fisher(0)

    hq_send(3)
    hq_relay(2)
    hq_wait(1)
    fisher(1)
    hq_send(4)
    hq_relay(3)
    hq_wait(2)
    fisher(2)
    hq_send(5)
    hq_relay(4)
    hq_wait(3)
    fisher(3)
    hq_relay(5)
    merge(0)
    rg_pass(1)
    squares(1)
    hq_wait(4)
    fisher(4)
    merge(1)
    hq_wait(5)
    fisher(5)
    for j in range(2, MERGED):
        merge(j)

    total = sib[z].astype(F32)
    for o in range(1, NZ):
        z_landed(o).wait_recv()
        total += zin[wrap(z - o)].astype(F32)
    us[...] = total.astype(BF)
    v_copy = remote(us.at[1 - yh], vin, v_s.at[0], v_r.at[0], y_mate)
    v_copy.start()

    for j in range(MERGED, PIECES):
        if j == PIECES - 1:
            v_copy.wait_recv()
            ig[0] = (us[yh].astype(F32) + vin[...].astype(F32)).astype(BF)
        merge(j)

    for a in range(2):
        yx_copy(a).wait_send()
        for u in range(2):
            for d in range(2):
                for s in range(1, 5):
                    if s < 4 or a == d:
                        ring_copy(a, d, s, u).wait_send()
        for slot in range(8):
            sib_fwd(a, z, slot).wait_send()
            zb = wrap(z + (0, -1, 1, -2, 2, -3, 3, 4)[slot])

            @pl.when(zb % NX != x)
            def _():
                xb_copy(a, zb, slot).wait_send()

        for o in range(1, NX):
            for half in range(2):
                rg_copy(a, o, half).wait_send()
    for i in range(3):
        w_copy(i).wait_send()
    for j in range(PIECES):
        f_copy(j).wait_send()
        for d in range(2):
            for hops in range(2):
                hq_copy(j, d, hops).wait_send()
    sib_part.wait_send()
    for o in range(1, NZ):
        z_copy(o).wait_send()
    v_copy.wait_send()


def hand_out(ig, mt, ig_out, mg, mu, md, sem):
    copies = [pltpu.make_async_copy(ig, ig_out, sem.at[3])]
    copies += [pltpu.make_async_copy(mt.at[i], (mg, mu, md)[i], sem.at[i]) for i in range(3)]
    for cp in copies:
        cp.start()
    for cp in copies:
        cp.wait()


def local(inputs, cotangent, gate_w, up_w, down_w):
    dma = pltpu.SemaphoreType.DMA
    vm = pltpu.VMEM
    ig, mt = pl.pallas_call(
        kernel,
        out_shape=(
            vm((1, TOK, FEAT), BF),
            vm((3, HID, ROWS), BF),
        ),
        in_specs=[pl.BlockSpec(memory_space=pl.ANY)] * 5,
        out_specs=[pl.BlockSpec(memory_space=pltpu.VMEM)] * 2,
        scratch_shapes=[
            vm((2, 2, NZ, 2, TOK, FEAT), BF),
            vm((2, 2, NX, 2, 2, TOK, FEAT), BF),
            vm((2, 2, NX * TOK, ROWS), BF),
            vm((3, NX, HID, TOK), BF),
            vm((3, HID, NZ * ROWS), BF),
            vm((3, HID, ROWS), BF),
            vm((3, HID, ROWS), BF),
            vm((3, HID, ROWS), BF),
            vm((3, HID, ROWS), BF),
            vm((3, HID, ROWS), BF),
            vm((2, NZ, 2, TOK, FEAT), BF),
            vm((NZ, 2, TOK, FEAT), BF),
            vm((NZ, 2, TOK, FEAT), BF),
            vm((2, TOK, FEAT), BF),
            vm((TOK, FEAT), BF),
            vm((3, HID, TOK), F32),
            vm((HID, TOK), BF),
            vm((HID, TOK), BF),
            vm((TOK, HID), BF),
            vm((TOK, HID), BF),
            dma((5,)),
            dma((2, 2, 5, 2)), dma((2, 2, 5, 2)),
            dma((2,)), dma((2,)),
            dma((2, 8)), dma((2, 8)),
            dma((2, 8)), dma((2, 3, 2)),
            dma((2, 3, 2)), dma((2, 3, 2)),
            dma((6, 2, 2)), dma((6, 2, 2)),
            dma((3,)), dma((3,)),
            dma((6,)), dma((6,)),
            dma((1,)), dma((1,)),
            dma((7,)), dma((7,)),
            dma((1,)), dma((1,)),
        ],
        compiler_params=pltpu.CompilerParams(collective_id=0, has_side_effects=True, vmem_limit_bytes=58 << 20),
        cost_estimate=pl.CostEstimate(flops=7_500_000_000, bytes_accessed=16_000_000, transcendentals=120_000),
        name="fisher_merge",
    )(inputs, cotangent, gate_w.swapaxes(1, 2), up_w.swapaxes(1, 2), down_w)
    ig, mg, mu, md = pl.pallas_call(
        hand_out,
        out_shape=(jax.ShapeDtypeStruct((1, TOK, FEAT), BF),) + (jax.ShapeDtypeStruct((HID, ROWS), BF),) * 3,
        in_specs=[pl.BlockSpec(memory_space=pltpu.VMEM)] * 2,
        out_specs=[pl.BlockSpec(memory_space=pl.ANY)] * 4,
        scratch_shapes=[dma((4,))],
        name="hand_out",
    )(*(pltpu.with_memory_space_constraint(v, pltpu.VMEM) for v in (ig, mt)))
    return ig, mg.T, mu.T, md


def solution(mesh):
    return jax.shard_map(
        local,
        mesh=mesh,
        in_specs=(
            P("mp", "token", "tensor"),
            P("mp", "token", "tensor"),
            P("mp", None, "tensor"),
            P("mp", None, "tensor"),
            P("mp", "tensor", None),
        ),
        out_specs=(
            P("mp", "token", "tensor"),
            P(("mp", "token"), "tensor"),
            P(("mp", "token"), "tensor"),
            P("tensor", ("mp", "token")),
        ),
        check_vma=False,
    )
```
